256 devices in a mesh: ctx: 64 (over x_lo, z, y), tp: 4 (over x_hi, core).
Axes of the slice: x: 4 (x_hi: 2, x_lo: 2; x = x_hi * 2 + x_lo), y: 4, z: 8, core: 2. Of those that a mesh axis runs over, the one named last changes fastest.
Arguments:
- queries: bfloat16 [8192, 4096], P('ctx', 'tp'), may hold values from -9 to 9
- key_rows: bfloat16 [8192, 512], P('ctx', 'tp'), may hold values from -6 to 6
- value_rows: bfloat16 [8192, 512], P('ctx', 'tp'), may hold values from -6 to 6
- attn_out: bfloat16 [8192, 4096], P('ctx', 'tp'), may hold values from -1.5 to 1.5
- log_norm: float32 [8192, 32], P('ctx', 'tp'), as said below
- grad_out: bfloat16 [8192, 4096], P(('ctx', 'tp')), may hold values from -6 to 6
- block_pos: int32 [128], replicated, may hold values from 0 to 127, as said below
Outputs:
- query_grad: bfloat16 [8192, 4096], P(('ctx', 'tp'))
- key_grad: bfloat16 [8192, 512], P(('ctx', 'tp'))
- value_grad: bfloat16 [8192, 512], P(('ctx', 'tp'))
The draws below stay inside these ranges and needn't reach their ends.
Inputs may be any that keep to these rules, and one draw needn't show every extreme that they name: `block_pos`: a permutation of 0 to 127. log_norm[i, h] lies between 0.8 and 1.6 above the natural logarithm of pos[i] + 1.
All inputs are finite; a program needn't handle non-finite values.
Results may differ from the reference program's by a relative error of at most 0.005.
Values may be sent and summed in bfloat16 or wider, within the bound.
A program may use at most 64 MiB of HBM per device.

```python
import math
import jax
import jax.numpy as jnp
from jax import lax

HEADS = 32
KV_HEADS = 4
HEAD_DIM = 128
TOK_DEV = 128
TOKENS = 8192
HALVES = 128


def shared_order(key):
    return jax.random.permutation(key, HALVES).astype(jnp.int32)


def draw_block_pos(key, part):
    return shared_order(key)


def draw_log_norm(key, part):
    order = shared_order(key)
    key = jax.random.fold_in(key, 5)
    half_rows = TOK_DEV // 2
    row_ids = jnp.arange(TOKENS, dtype=jnp.int32)
    places = order[row_ids // half_rows] * half_rows + row_ids % half_rows
    base = jnp.log(places.astype(jnp.float32) + 1.0)
    return base[:, None] + jax.random.uniform(key, (TOKENS, HEADS), jnp.float32, 0.8, 1.6)


def level_of(rng, dims, pieces, low, top_value):
    level = 1.0
    for axis_at, parts in pieces:
        draws = jax.random.uniform(jax.random.fold_in(jax.random.fold_in(rng, 6), axis_at), (parts,), jnp.float32, low / len(pieces), top_value / len(pieces))
        level = level * jnp.repeat(jnp.exp(draws), dims[axis_at] // parts).reshape((-1,) + (1,) * (len(dims) - 1 - axis_at))
    return level


def bell_draw(own_key, extent, spread, reach, shards=(), held_as=jnp.bfloat16):
    array = jax.random.normal(own_key, extent, jnp.float32) * spread
    if len(shards) > 0:
        array = level_of(own_key, extent, shards, -0.22, 0.18) * array
    return jnp.clip(array, min=-reach, max=reach).astype(held_as)


def setup_inputs(seed: int = 0) -> dict:
    keys = jax.random.split(jax.random.key(seed), 8)
    queries = bell_draw(keys[0], (TOKENS, HEADS * HEAD_DIM), 1.5, 9.0, ((0, 64), (1, 4)))
    key_rows = bell_draw(keys[1], (TOKENS, KV_HEADS * HEAD_DIM), 1.0, 6.0, ((0, 64), (1, 4)))
    value_rows = bell_draw(keys[2], (TOKENS, KV_HEADS * HEAD_DIM), 1.0, 6.0, ((0, 64), (1, 4)))
    attn_out = bell_draw(keys[3], (TOKENS, HEADS * HEAD_DIM), 0.25, 1.5, ((0, 64), (1, 4)))
    log_norm = draw_log_norm(jax.random.fold_in(keys[7], 71), 0)
    grad_out = bell_draw(keys[5], (TOKENS, HEADS * HEAD_DIM), 1.0, 6.0, ((0, 256),))
    block_pos = draw_block_pos(jax.random.fold_in(keys[7], 71), 0)
    return {"queries": queries, "key_rows": key_rows, "value_rows": value_rows, "attn_out": attn_out, "log_norm": log_norm, "grad_out": grad_out, "block_pos": block_pos}


def rounded(value):
    return lax.optimization_barrier(value.astype(jnp.bfloat16)).astype(jnp.float32)


def reference(queries, key_rows, value_rows, attn_out, log_norm, grad_out, block_pos):
    half_rows = TOK_DEV // 2
    group_size = HEADS // KV_HEADS
    scaling = HEAD_DIM ** -0.5
    offsets = jnp.arange(half_rows, dtype=jnp.int32)
    positions = (block_pos.astype(jnp.int32)[:, None] * half_rows + offsets[None, :]).reshape(-1)
    query_all = queries.astype(jnp.float32).reshape(TOKENS, KV_HEADS, group_size, HEAD_DIM).transpose(1, 0, 2, 3)
    grad_all = grad_out.astype(jnp.float32).reshape(TOKENS, KV_HEADS, group_size, HEAD_DIM).transpose(1, 0, 2, 3)
    out_all = attn_out.astype(jnp.float32).reshape(TOKENS, KV_HEADS, group_size, HEAD_DIM).transpose(1, 0, 2, 3)
    deltas = jnp.sum(grad_all * out_all, axis=-1)
    norms = log_norm.reshape(TOKENS, KV_HEADS, group_size).transpose(1, 0, 2)
    key_all = key_rows.astype(jnp.float32).reshape(TOKENS, KV_HEADS, HEAD_DIM).transpose(1, 0, 2)
    value_all = value_rows.astype(jnp.float32).reshape(TOKENS, KV_HEADS, HEAD_DIM).transpose(1, 0, 2)
    block_len = math.gcd(TOKENS, 512)
    begins = jnp.arange(TOKENS // block_len, dtype=jnp.int32) * block_len

    def per_group(packed):
        query_g, grad_g, delta_g, norm_g, key_g, value_g = packed

        def per_block(carried, begin_row):
            key_acc, value_acc = carried
            query_b = lax.dynamic_slice_in_dim(query_g, begin_row, block_len, 0)
            grad_b = lax.dynamic_slice_in_dim(grad_g, begin_row, block_len, 0)
            delta_b = lax.dynamic_slice_in_dim(delta_g, begin_row, block_len, 0).T
            norm_b = lax.dynamic_slice_in_dim(norm_g, begin_row, block_len, 0).T
            query_pos = lax.dynamic_slice_in_dim(positions, begin_row, block_len, 0)
            scores = jnp.einsum("rgd,nd->grn", query_b, key_g) * scaling
            allowed = query_pos[:, None] >= positions[None, :]
            attn_prob = jnp.where(allowed[None], jnp.exp(scores - norm_b[:, :, None]), 0.0)
            prob_grad = jnp.einsum("rgd,nd->grn", grad_b, value_g)
            score_grad = rounded(attn_prob * (prob_grad - delta_b[:, :, None]))
            value_acc = value_acc + jnp.einsum("grn,rgd->nd", rounded(attn_prob), grad_b)
            key_acc = key_acc + jnp.einsum("grn,rgd->nd", score_grad, query_b)
            query_part = jnp.einsum("grn,nd->rgd", score_grad, key_g)
            return (key_acc, value_acc), query_part

        zero_acc = jnp.zeros((TOKENS, HEAD_DIM), jnp.float32)
        (key_acc, value_acc), query_parts = lax.scan(per_block, (zero_acc, zero_acc), begins)
        return query_parts.reshape(TOKENS, group_size, HEAD_DIM), key_acc, value_acc

    query_sum, key_sum, value_sum = lax.map(per_group, (query_all, grad_all, deltas, norms, key_all, value_all))
    query_grad = (query_sum.transpose(1, 0, 2, 3).reshape(TOKENS, HEADS * HEAD_DIM) * scaling).astype(jnp.bfloat16)
    key_grad = (key_sum.transpose(1, 0, 2).reshape(TOKENS, KV_HEADS * HEAD_DIM) * scaling).astype(jnp.bfloat16)
    value_grad = value_sum.transpose(1, 0, 2).reshape(TOKENS, KV_HEADS * HEAD_DIM).astype(jnp.bfloat16)
    return (query_grad, key_grad, value_grad)
```

```python
import functools

import jax
import jax.numpy as jnp
from jax import lax
from jax.experimental import pallas as pl
from jax.experimental.pallas import tpu as pltpu
from jax.sharding import PartitionSpec as P

MESH = pl.DeviceIdType.MESH
HEAD_DIM = 128
GROUP = 8
TOK = 128
NX, NZ, NY, NT = 2, 8, 4, 4
ROWS = GROUP * TOK
SCALE = HEAD_DIM ** -0.5
LOG2E = 1.4426950408889634
NEG = -32768.0
BF = jnp.bfloat16
F32 = jnp.float32


def mm(a, b, dims):
    return lax.dot_general(a, b, (dims, ((), ())), preferred_element_type=F32)


def unit_order():
    order = [(0, 0), (-1, 0)] + ([(1, 0)] if NZ > 2 else [])
    order += [(0, 1), (-1, 1)] + ([(1, 1)] if NZ > 2 else [])
    for dist in range(2, NZ // 2 + 1):
        order += [(-dist, 0), (-dist, 1)]
        if dist < NZ // 2:
            order += [(dist, 0), (dist, 1)]
    return order


def pick(index, table):
    value = jnp.int32(table[0])
    for at, entry in enumerate(table):
        if at:
            value = jnp.where(index == at, jnp.int32(entry), value)
    return value


def split3(x):
    hi = x.astype(BF).astype(F32)
    mid = (x - hi).astype(BF).astype(F32)
    return hi, mid, x - hi - mid


def kernel(
    q_in, k_in, v_in, o_in, ln_in, do_in, bp,
    dq_out, dk_out, dv_out,
    kv, q2, dobuf, ld, qrow, dorow, qt, dot, dqt, acc, sendbuf, red1, s2buf, red2, fkv, rkv, dqs, rdq, kaug,
    kvy_s, kvy_r, do_s, do_r, q_s, q_r, ld_s, ld_r, f_s, f_r, b_s, b_r, s1_s, s1_r, s2_s, s2_r, kv_s, kv_r, dq_s, dq_r,
):
    ctx = lax.axis_index("ctx")
    t = lax.axis_index("tp")
    plane = NZ * NY
    xl = lax.div(ctx, plane)
    z = lax.rem(lax.div(ctx, NY), NZ)
    y = lax.rem(ctx, NY)
    xp = 1 - xl
    piece = TOK // NT

    def dev(x_, z_, y_, t_):
        return (x_ * plane + z_ * NY + y_, t_)

    def wrap(value, count):
        return lax.rem(value + count, count)

    group = [(dx, dt) for dx in range(NX) for dt in range(NT) if dx or dt]

    def group_dev(dx, dt):
        return dev(lax.rem(xl + dx, NX), z, y, lax.rem(t + dt, NT))

    barrier = pltpu.get_barrier_semaphore()
    peers = [group_dev(dx, dt) for dx, dt in group]
    peers += [dev(xl, z, lax.rem(y + dy, NY), t) for dy in range(1, NY)]
    peers += [dev(xl, lax.rem(z + dz, NZ), y, t) for dz in range(1, NZ)]
    for peer in peers:
        pl.semaphore_signal(barrier, inc=1, device_id=peer, device_id_type=MESH)
    pl.semaphore_wait(barrier, len(peers))

    def copy(src, dst, send, recv, device):
        return pltpu.make_async_remote_copy(
            src_ref=src, dst_ref=dst, send_sem=send, recv_sem=recv, device_id=device, device_id_type=MESH
        )

    def do_copy(dx, dt):
        tt = lax.rem(t + dt, NT)
        n = dx * NT + dt
        return copy(
            do_in.at[:, pl.ds(pl.multiple_of(tt * ROWS, ROWS), ROWS)],
            dobuf.at[dx, pl.ds(pl.multiple_of(t * piece, piece), piece), :],
            do_s.at[n], do_r.at[n], group_dev(dx, dt),
        )

    def kvy_copy(dy):
        return copy(kv.at[z, y], kv.at[z, y], kvy_s.at[dy], kvy_r.at[dy], dev(xl, z, lax.rem(y + dy, NY), t))

    def q_copy():
        return copy(q_in, q2, q_s.at[0], q_r.at[0], dev(xp, z, y, t))

    def ld_copy():
        return copy(ld.at[0], ld.at[1], ld_s.at[0], ld_r.at[0], dev(xp, z, y, t))

    def f_copy(step):
        row = wrap(z - step, NZ)
        return copy(kv.at[row], kv.at[row], f_s.at[step], f_r.at[step], dev(xl, lax.rem(z + 1, NZ), y, t))

    def b_copy(step):
        row = lax.rem(z + step, NZ)
        return copy(kv.at[row], kv.at[row], b_s.at[step], b_r.at[step], dev(xl, wrap(z - 1, NZ), y, t))

    def s1_copy(row, dy):
        yy = lax.rem(y + dy, NY)
        return copy(
            sendbuf.at[row, yy], red1.at[row, y], s1_s.at[row, dy], s1_r.at[row, dy], dev(xl, z, yy, t)
        )

    def s2_copy(row):
        return copy(s2buf.at[row], red2.at[z], s2_s.at[row], s2_r.at[z], dev(xl, row, y, t))

    def kvo_copy(dt):
        tt = lax.rem(t + dt, NT)
        rows = pl.ds(pl.multiple_of(tt * piece, piece), piece)
        return copy(fkv.at[:, rows, :], rkv.at[t], kv_s.at[dt], kv_r.at[dt], dev(xl, z, y, tt))

    def dq_copy(dx, dt):
        tt = lax.rem(t + dt, NT)
        n = dx * NT + dt
        rows = pl.ds(pl.multiple_of(tt * piece, piece), piece)
        return copy(dqs.at[dx, rows, :], rdq.at[dx, t], dq_s.at[n], dq_r.at[n], group_dev(dx, dt))

    for dt in range(1, NT):
        do_copy(0, dt).start()
    kv[z, y, 0] = k_in[...]
    kv[z, y, 1] = v_in[...]
    for dy in range(1, NY):
        kvy_copy(dy).start()
    for dt in range(NT):
        do_copy(1, dt).start()
    q_copy().start()
    dobuf[0, pl.ds(pl.multiple_of(t * piece, piece), piece), :] = do_in[
        :, pl.ds(pl.multiple_of(t * ROWS, ROWS), ROWS)
    ]

    sub16 = lax.broadcasted_iota(jnp.int32, (16, TOK), 0)
    tok16 = lax.broadcasted_iota(jnp.int32, (16, TOK), 1)

    def put_heads(half, src, rows_ref, cols_ref):
        for h in range(GROUP):
            blk = src[:, h * HEAD_DIM:(h + 1) * HEAD_DIM]
            at = slice(half * ROWS + h * TOK, half * ROWS + (h + 1) * TOK)
            rows_ref[at, :] = blk
            cols_ref[:HEAD_DIM, at] = blk.T

    def put_extra(half, base, cols_ref, hot):
        for h in range(GROUP):
            hi, mid, low = split3(ld[half, base + h:base + h + 1, :])
            tile = jnp.where(sub16 == 4 + 2 * half + tok16 // (TOK // 2), hot, 0.0)
            tile = jnp.where(sub16 == 0, hi, jnp.where(sub16 == 1, mid, jnp.where(sub16 == 2, low, tile)))
            at = slice(half * ROWS + h * TOK, half * ROWS + (h + 1) * TOK)
            cols_ref[HEAD_DIM:HEAD_DIM + 16, at] = tile.astype(BF)

    acc[...] = jnp.zeros_like(acc)
    dqt[...] = jnp.zeros_like(dqt)
    qt[HEAD_DIM:, :] = jnp.zeros_like(qt[HEAD_DIM:, :])
    dot[HEAD_DIM:, :] = jnp.zeros_like(dot[HEAD_DIM:, :])
    ld[0, :GROUP, :] = ln_in[...].T * (-1.0 / SCALE)
    put_heads(0, q_in, qrow, qt)
    put_extra(0, 0, qt, 1.0)

    lane = lax.broadcasted_iota(jnp.int32, (1, HEAD_DIM), 1)
    here, there = 2 * ctx, 2 * (xp * plane + z * NY + y)
    limit = jnp.full((1, HEAD_DIM), 1 << 20, jnp.int32)
    for at, half_block in enumerate((here, here + 1, there, there + 1)):
        limit = jnp.where(lane == 4 + at, bp[half_block], limit)

    def put_kaug(row, carry):
        for yy in range(NY):
            for hf in range(2):
                place = bp[2 * (xl * plane + row * NY + yy) + hf]
                line = jnp.where(lane < 3, 1.0, jnp.where(place > limit, NEG, 0.0))
                kaug[row, yy * TOK + hf * (TOK // 2):yy * TOK + (hf + 1) * (TOK // 2), :] = jnp.broadcast_to(
                    line, (TOK // 2, HEAD_DIM)
                ).astype(BF)
        return carry

    lax.fori_loop(0, NZ, put_kaug, 0)

    for dt in range(1, NT):
        do_copy(0, dt).wait_recv()
    put_heads(0, dobuf.at[0], dorow, dot)
    for h in range(GROUP):
        out_t = o_in[:, h * HEAD_DIM:(h + 1) * HEAD_DIM].T.astype(F32)
        grad_t = dot[:HEAD_DIM, h * TOK:(h + 1) * TOK].astype(F32)
        ld[0, GROUP + h:GROUP + h + 1, :] = -jnp.sum(out_t * grad_t, axis=0, keepdims=True)
    ld_copy().start()
    put_extra(0, GROUP, dot, 0.0)

    for dy in range(1, NY):
        kvy_copy(dy).wait_recv()
    f_copy(0).start()
    if NZ > 2:
        b_copy(0).start()

    n_keys = NY * TOK
    ones = jnp.where(lax.broadcasted_iota(jnp.int32, (n_keys, HEAD_DIM), 1) < 3, 1.0, 0.0).astype(BF)

    def unit(row, half, diagonal):
        cols = pl.ds(pl.multiple_of(half * ROWS, ROWS), ROWS)
        keys = kv[row, :, 0].reshape(n_keys, HEAD_DIM)
        values = kv[row, :, 1].reshape(n_keys, HEAD_DIM)
        s = mm(jnp.concatenate([keys, kaug[row]], axis=1), qt[:, cols], ((1,), (0,)))
        p = jnp.exp2(s * (SCALE * LOG2E))
        if diagonal:
            key_at = lax.broadcasted_iota(jnp.int32, (n_keys, ROWS), 0) - y * TOK
            query_at = lax.broadcasted_iota(jnp.int32, (n_keys, ROWS), 1) % TOK
            p = jnp.where((key_at > query_at) & (key_at <= (query_at | (TOK // 2 - 1))), 0.0, p)
        dp = mm(jnp.concatenate([values, ones], axis=1), dot[:, cols], ((1,), (0,)))
        ds = (p * dp).astype(BF)
        acc[row, 1] += mm(p.astype(BF), dorow[cols, :], ((1,), (0,)))
        acc[row, 0] += mm(ds, qrow[cols, :], ((1,), (0,)))
        dqt[:, cols] += mm(keys, ds, ((0,), (0,)))

    def send_row(row):
        for yy in range(NY):
            sendbuf[row, yy] = acc[row, :, yy * TOK:(yy + 1) * TOK, :].astype(BF)
        for dy in range(1, NY):
            s1_copy(row, dy).start()

    def sum_row(row, own):
        for dy in range(1, NY):
            s1_copy(row, dy).wait_recv()
        total = acc[row, :, pl.ds(pl.multiple_of(y * TOK, TOK), TOK), :]
        for dy in range(1, NY):
            total = total + red1[row, lax.rem(y + dy, NY)].astype(F32)
        if own:
            acc[row, :, pl.ds(pl.multiple_of(y * TOK, TOK), TOK), :] = total
        else:
            s2buf[row] = total.astype(BF)
            s2_copy(row).start()

    order = unit_order()
    rels, halves = [r for r, _ in order], [h for _, h in order]
    seen, done_at = set(), {}
    for at, (rel, _) in enumerate(order):
        if rel in seen:
            done_at[rel] = at
        seen.add(rel)
    finished = sorted(done_at, key=done_at.get)
    first_partner = halves.index(1)

    unit(z, 0, True)

    def step(u, carry):
        row = wrap(z + pick(u, rels), NZ)
        half = pick(u, halves)

        for dist in range(1, NZ // 2 + 1):
            @pl.when(u == rels.index(-dist))
            def _():
                f_copy(dist - 1).wait_recv()
                if dist < NZ // 2:
                    f_copy(dist).start()
                    b_copy(dist - 1).wait_recv()
                    if dist < NZ // 2 - 1:
                        b_copy(dist).start()

        @pl.when(u == first_partner)
        def _():
            for dt in range(NT):
                do_copy(1, dt).wait_recv()
            q_copy().wait_recv()
            ld_copy().wait_recv()
            put_heads(1, q2, qrow, qt)
            put_extra(1, 0, qt, 1.0)
            put_heads(1, dobuf.at[1], dorow, dot)
            put_extra(1, GROUP, dot, 0.0)

        unit(row, half, False)

        @pl.when(half == 1)
        def _():
            send_row(row)

        for at, rel in enumerate(finished[:-1]):
            @pl.when(u == done_at[finished[at + 1]])
            def _():
                sum_row(wrap(z + rel, NZ), rel == 0)

        return carry

    lax.fori_loop(1, len(order), step, 0)

    for half in (1, 0):
        for h in range(GROUP):
            at = slice(half * ROWS + h * TOK, half * ROWS + (h + 1) * TOK)
            dqs[half, :, h * HEAD_DIM:(h + 1) * HEAD_DIM] = (dqt[:, at].T * SCALE).astype(BF)
        for dt in range(NT):
            if half or dt:
                dq_copy(half, dt).start()
    rdq[0, t] = dqs[0, pl.ds(pl.multiple_of(t * piece, piece), piece), :]

    sum_row(wrap(z + finished[-1], NZ), False)
    total = acc[z, :, pl.ds(pl.multiple_of(y * TOK, TOK), TOK), :]
    for dz in range(1, NZ):
        s2_copy_back = copy(
            s2buf.at[z], red2.at[lax.rem(z + dz, NZ)], s2_s.at[z], s2_r.at[lax.rem(z + dz, NZ)], dev(xl, z, y, t)
        )
        s2_copy_back.wait_recv()
        total = total + red2[lax.rem(z + dz, NZ)].astype(F32)
    fkv[0] = (total[0] * SCALE).astype(BF)
    fkv[1] = total[1].astype(BF)
    for dt in range(1, NT):
        kvo_copy(dt).start()
    rkv[t] = fkv[:, pl.ds(pl.multiple_of(t * piece, piece), piece), :]

    for dx, dt in group:
        dq_copy(dx, dt).wait_recv()
    for tt in range(NT):
        dq_out[:, tt * ROWS:(tt + 1) * ROWS] = (rdq[0, tt].astype(F32) + rdq[1, tt].astype(F32)).astype(BF)
    for dt in range(1, NT):
        kvo_copy(dt).wait_recv()
    for tt in range(NT):
        dk_out[:, tt * HEAD_DIM:(tt + 1) * HEAD_DIM] = rkv[tt, 0]
        dv_out[:, tt * HEAD_DIM:(tt + 1) * HEAD_DIM] = rkv[tt, 1]

    for dx, dt in group:
        do_copy(dx, dt).wait_send()
        dq_copy(dx, dt).wait_send()
    for dy in range(1, NY):
        kvy_copy(dy).wait_send()
    q_copy().wait_send()
    ld_copy().wait_send()
    for s in range(NZ // 2):
        f_copy(s).wait_send()
    for s in range(NZ // 2 - 1):
        b_copy(s).wait_send()
    for dz in range(NZ):
        row = lax.rem(z + dz, NZ)
        for dy in range(1, NY):
            s1_copy(row, dy).wait_send()
        if dz:
            s2_copy(row).wait_send()
    for dt in range(1, NT):
        kvo_copy(dt).wait_send()


def per_device(queries, key_rows, value_rows, attn_out, log_norm, grad_out, block_pos):
    piece = TOK // NT
    vmem = pl.BlockSpec(memory_space=pltpu.VMEM)
    dma = pltpu.SemaphoreType.DMA
    blk = (2, TOK, HEAD_DIM)
    return pl.pallas_call(
        kernel,
        out_shape=[
            jax.ShapeDtypeStruct((piece, NT * ROWS), BF),
            jax.ShapeDtypeStruct((piece, NT * HEAD_DIM), BF),
            jax.ShapeDtypeStruct((piece, NT * HEAD_DIM), BF),
        ],
        in_specs=[vmem] * 6 + [pl.BlockSpec(memory_space=pltpu.SMEM)],
        out_specs=[vmem] * 3,
        scratch_shapes=[
            pltpu.VMEM((NZ, NY) + blk, BF),
            pltpu.VMEM((TOK, ROWS), BF),
            pltpu.VMEM((2, TOK, ROWS), BF),
            pltpu.VMEM((2, 2 * GROUP, TOK), F32),
            pltpu.VMEM((2 * ROWS, HEAD_DIM), BF),
            pltpu.VMEM((2 * ROWS, HEAD_DIM), BF),
            pltpu.VMEM((2 * HEAD_DIM, 2 * ROWS), BF),
            pltpu.VMEM((2 * HEAD_DIM, 2 * ROWS), BF),
            pltpu.VMEM((HEAD_DIM, 2 * ROWS), F32),
            pltpu.VMEM((NZ, 2, NY * TOK, HEAD_DIM), F32),
            pltpu.VMEM((NZ, NY) + blk, BF),
            pltpu.VMEM((NZ, NY) + blk, BF),
            pltpu.VMEM((NZ,) + blk, BF),
            pltpu.VMEM((NZ,) + blk, BF),
            pltpu.VMEM(blk, BF),
            pltpu.VMEM((NT, 2, piece, HEAD_DIM), BF),
            pltpu.VMEM((2, TOK, ROWS), BF),
            pltpu.VMEM((2, NT, piece, ROWS), BF),
            pltpu.VMEM((NZ, NY * TOK, HEAD_DIM), BF),
            dma((NY,)), dma((NY,)), dma((2 * NT,)), dma((2 * NT,)), dma((1,)), dma((1,)), dma((1,)), dma((1,)),
            dma((NZ // 2,)), dma((NZ // 2,)), dma((NZ // 2,)), dma((NZ // 2,)), dma((NZ, NY)), dma((NZ, NY)),
            dma((NZ,)), dma((NZ,)), dma((NT,)), dma((NT,)), dma((2 * NT,)), dma((2 * NT,)),
        ],
        compiler_params=pltpu.CompilerParams(
            collective_id=0, has_side_effects=True, vmem_limit_bytes=52 * 2**20
        ),
    )(queries, key_rows, value_rows, attn_out, log_norm, grad_out, block_pos)


def solution(mesh):
    split = P("ctx", "tp")
    joint = P(("ctx", "tp"), None)
    return jax.shard_map(
        per_device,
        mesh=mesh,
        in_specs=(split, split, split, split, split, joint, P()),
        out_specs=(joint, joint, joint),
        check_vma=False,
    )
```

```python
import functools

import jax
import jax.numpy as jnp
from jax import lax
from jax.experimental import pallas as pl
from jax.experimental.pallas import tpu as pltpu
from jax.sharding import PartitionSpec as P

MESH = pl.DeviceIdType.MESH
HEAD_DIM = 128
GROUP = 8
TOK = 128
NX, NZ, NY, NT = 2, 8, 4, 4
LAG = 3
ROWS = GROUP * TOK
SCALE = HEAD_DIM ** -0.5
LOG2E = 1.4426950408889634
NEG = -32768.0
BF = jnp.bfloat16
F32 = jnp.float32


def mm(a, b, dims):
    return lax.dot_general(a, b, (dims, ((), ())), preferred_element_type=F32)


def unit_order():
    if NZ != 8:
        rels = [0] + [rel for d in range(1, NZ // 2 + 1) for rel in ((-d, d) if d < NZ // 2 else (-d,))]
        return [(rel, half) for half in range(2) for rel in (rels, rels[::-1])[half]]
    near = [(0, 0), (-1, 0), (1, 0), (-1, 1), (-2, 0), (2, 0), (-2, 1), (2, 1)]
    return near + [(-3, 0), (3, 0), (-3, 1), (3, 1), (-4, 0), (-4, 1), (1, 1), (0, 1)]


def pick(index, table):
    value = jnp.int32(table[0])
    for at, entry in enumerate(table):
        if at:
            value = jnp.where(index == at, jnp.int32(entry), value)
    return value


def split3(x):
    hi = x.astype(BF).astype(F32)
    mid = (x - hi).astype(BF).astype(F32)
    return hi, mid, x - hi - mid


def kernel(
    q_hbm, k_in, v_in, o_hbm, ln_in, do_in, bp_in,
    dq_out, dk_out, dv_out,
    q_in, o_in, bp, kk, vv, q2, dobuf, ld, qrow, dorow, qt, dot, dqt, acc, sendbuf, red1, s2buf, fin, dqs, rdq, kaug,
    loc, ky_s, ky_r, vz_s, vz_r, vy_s, vy_r, do_s, do_r, q_s, q_r, ld_s, ld_r, ring_s, ring_r, s1_s, s1_r, s2_s, s2_r, kv_s, kv_r, dq_s, dq_r,
):
    ctx = lax.axis_index("ctx")
    t = lax.axis_index("tp")
    plane = NZ * NY
    xl = lax.div(ctx, plane)
    z = lax.rem(lax.div(ctx, NY), NZ)
    y = lax.rem(ctx, NY)
    xp = 1 - xl
    piece = TOK // NT

    def dev(x_, z_, y_, t_):
        return (x_ * plane + z_ * NY + y_, t_)

    def wrap(value, count):
        return lax.rem(value + count, count)

    group = [(dx, dt) for dx in range(NX) for dt in range(NT) if dx or dt]

    def group_dev(dx, dt):
        return dev(lax.rem(xl + dx, NX), z, y, lax.rem(t + dt, NT))

    barrier = pltpu.get_barrier_semaphore()
    peers = [group_dev(dx, dt) for dx, dt in group]
    peers += [dev(xl, z, lax.rem(y + dy, NY), t) for dy in range(1, NY)]
    peers += [dev(xl, lax.rem(z + dz, NZ), y, t) for dz in range(1, NZ)]
    for peer in peers:
        pl.semaphore_signal(barrier, inc=1, device_id=peer, device_id_type=MESH)

    fetches = [
        pltpu.make_async_copy(src, dst, loc.at[at])
        for at, (src, dst) in enumerate([
            (k_in, kk.at[z, 0]),
            (v_in, vv.at[z, 0]),
            (q_hbm, q_in),
            (ln_in, ld.at[0, :GROUP, :]),
            (bp_in, bp),
            (o_hbm, o_in),
            (
                do_in.at[:, pl.ds(pl.multiple_of(t * ROWS, ROWS), ROWS)],
                dobuf.at[0, pl.ds(pl.multiple_of(t * piece, piece), piece), :],
            ),
        ])
    ]
    for fetch in fetches:
        fetch.start()
    pl.semaphore_wait(barrier, len(peers))

    def copy(src, dst, send, recv, device):
        return pltpu.make_async_remote_copy(
            src_ref=src, dst_ref=dst, send_sem=send, recv_sem=recv, device_id=device, device_id_type=MESH
        )

    def settle(ref, sem):
        pltpu.make_async_copy(ref, ref, sem).wait()

    def do_copy(dx, dt):
        tt = lax.rem(t + dt, NT)
        return copy(
            do_in.at[:, pl.ds(pl.multiple_of(tt * ROWS, ROWS), ROWS)],
            dobuf.at[dx, pl.ds(pl.multiple_of(t * piece, piece), piece), :],
            do_s.at[dx], do_r.at[dx], group_dev(dx, dt),
        )

    def ky_copy(dy):
        return copy(kk.at[z, 0], kk.at[z, dy], ky_s.at[0], ky_r.at[0], dev(xl, z, lax.rem(y + dy, NY), t))

    def vz_copy(dz):
        dist = min(dz, NZ - dz)
        return copy(vv.at[z, 0], vv.at[z, 0], vz_s.at[0], vz_r.at[dist], dev(xl, lax.rem(z + dz, NZ), y, t))

    def vy_copy(row, dy):
        return copy(vv.at[row, 0], vv.at[row, dy], vy_s.at[0], vy_r.at[row], dev(xl, z, lax.rem(y + dy, NY), t))

    def q_copy():
        return copy(q_hbm, q2, q_s.at[0], q_r.at[0], dev(xp, z, y, t))

    def ld_copy():
        return copy(ld.at[0], ld.at[1], ld_s.at[0], ld_r.at[0], dev(xp, z, y, t))

    def ring_copy(step, back):
        row = lax.rem(z + step, NZ) if back else wrap(z - step, NZ)
        to = wrap(z - 1, NZ) if back else lax.rem(z + 1, NZ)
        part = pl.ds(0, NY) if step < NZ // 2 - 1 else pl.ds(back * NY // 2, NY // 2)
        return copy(kk.at[row, part], kk.at[row, part], ring_s.at[0], ring_r.at[step], dev(xl, to, y, t))

    def s1_copy(row, dy):
        return copy(
            sendbuf.at[row, dy - 1], red1.at[row, dy - 1], s1_s.at[0], s1_r.at[row], dev(xl, z, wrap(y - dy, NY), t)
        )

    def s2_copy(row, dt):
        tt = lax.rem(t + dt, NT)
        rows = pl.ds(pl.multiple_of(tt * piece, piece), piece)
        from_there = wrap(z - row, NZ) - 1
        return copy(s2buf.at[row, :, rows, :], fin.at[from_there, t], s2_s.at[0], s2_r.at[0], dev(xl, row, y, tt))

    def own_copy(dy, dt):
        tt = lax.rem(t + dt, NT)
        rows = pl.ds(pl.multiple_of(tt * piece, piece), piece)
        src = sendbuf.at[z, dy - 1, :, rows, :] if dy else s2buf.at[z, :, rows, :]
        n = min(dy, 1)
        return copy(src, fin.at[NZ - 1 + dy, t], kv_s.at[n], kv_r.at[n], dev(xl, z, wrap(y - dy, NY), tt))

    def dq_copy(dx, dt):
        tt = lax.rem(t + dt, NT)
        rows = pl.ds(pl.multiple_of(tt * piece, piece), piece)
        return copy(dqs.at[dx, rows, :], rdq.at[dx, t], dq_s.at[dx], dq_r.at[dx], group_dev(dx, dt))

    for dt in range(1, NT):
        do_copy(0, dt).start()
    fetches[0].wait()
    fetches[1].wait()

    for dy in range(1, NY):
        ky_copy(dy).start()
    near_first = [dz for _, dz in sorted((min(dz, NZ - dz), dz) for dz in range(1, NZ))]
    for dy in range(1, NY):
        vy_copy(z, dy).start()
    for dz in near_first[:2]:
        vz_copy(dz).start()

    sub16 = lax.broadcasted_iota(jnp.int32, (16, TOK), 0)
    tok16 = lax.broadcasted_iota(jnp.int32, (16, TOK), 1)

    def put_heads(half, src, rows_ref, cols_ref):
        for h in range(GROUP):
            blk = src[:, h * HEAD_DIM:(h + 1) * HEAD_DIM]
            at = slice(half * ROWS + h * TOK, half * ROWS + (h + 1) * TOK)
            rows_ref[at, :] = blk
            cols_ref[:HEAD_DIM, at] = blk.T

    def put_extra(half, base, cols_ref, hot):
        for h in range(GROUP):
            hi, mid, low = split3(ld[half, base + h:base + h + 1, :])
            tile = jnp.where(sub16 == 4 + 2 * half + tok16 // (TOK // 2), hot, 0.0)
            tile = jnp.where(sub16 == 0, hi, jnp.where(sub16 == 1, mid, jnp.where(sub16 == 2, low, tile)))
            at = slice(half * ROWS + h * TOK, half * ROWS + (h + 1) * TOK)
            cols_ref[HEAD_DIM:HEAD_DIM + 16, at] = tile.astype(BF)

    acc[...] = jnp.zeros_like(acc)
    dqt[...] = jnp.zeros_like(dqt)
    qt[HEAD_DIM:, :] = jnp.zeros_like(qt[HEAD_DIM:, :])
    dot[HEAD_DIM:, :] = jnp.zeros_like(dot[HEAD_DIM:, :])
    for fetch in fetches[2:5]:
        fetch.wait()
    ld[0, :GROUP, :] = ld[0, :GROUP, :] * (-1.0 / SCALE)
    put_heads(0, q_in, qrow, qt)
    put_extra(0, 0, qt, 1.0)

    lane = lax.broadcasted_iota(jnp.int32, (1, HEAD_DIM), 1)
    here, there = 2 * ctx, 2 * (xp * plane + z * NY + y)
    limit = jnp.full((1, HEAD_DIM), 1 << 20, jnp.int32)
    for at, half_block in enumerate((here, here + 1, there, there + 1)):
        limit = jnp.where(lane == 4 + at, bp[half_block], limit)

    def put_kaug(row, carry):
        for yy in range(NY):
            for hf in range(2):
                place = bp[2 * (xl * plane + row * NY + wrap(y - yy, NY)) + hf]
                line = jnp.where(lane < 3, 1.0, jnp.where(place > limit, NEG, 0.0))
                kaug[row, yy * TOK + hf * (TOK // 2):yy * TOK + (hf + 1) * (TOK // 2), :] = jnp.broadcast_to(
                    line, (TOK // 2, HEAD_DIM)
                ).astype(BF)
        return carry

    lax.fori_loop(0, NZ, put_kaug, 0)
    for dt in range(NT):
        do_copy(1, dt).start()
    q_copy().start()
    for dz in near_first[2:]:
        vz_copy(dz).start()

    settle(kk.at[z, 1:], ky_r.at[0])
    ring_copy(0, 0).start()
    ring_copy(0, 1).start()

    def pass_values(dist):
        both = sorted({dist, NZ - dist})
        settle(vv.at[:len(both), 0], vz_r.at[dist])
        for dz in both:
            for dy in range(1, NY):
                vy_copy(wrap(z - dz, NZ), dy).start()

    def pass_keys(dist):
        settle(kk.at[:2 if dist < NZ // 2 else 1], ring_r.at[dist - 1])
        if dist < NZ // 2:
            ring_copy(dist, 0).start()
            ring_copy(dist, 1).start()

    pass_values(1)
    pass_keys(1)
    for fetch in fetches[5:]:
        fetch.wait()
    if NT > 1:
        settle(dobuf.at[0, :(NT - 1) * piece], do_r.at[0])
    put_heads(0, dobuf.at[0], dorow, dot)
    for h in range(GROUP):
        out_t = o_in[:, h * HEAD_DIM:(h + 1) * HEAD_DIM].T.astype(F32)
        grad_t = dot[:HEAD_DIM, h * TOK:(h + 1) * TOK].astype(F32)
        ld[0, GROUP + h:GROUP + h + 1, :] = -jnp.sum(out_t * grad_t, axis=0, keepdims=True)
    ld_copy().start()
    put_extra(0, GROUP, dot, 0.0)

    n_keys = NY * TOK
    ones = jnp.where(lax.broadcasted_iota(jnp.int32, (n_keys, HEAD_DIM), 1) < 3, 1.0, 0.0).astype(BF)

    def unit(row, half, diagonal):
        cols = pl.ds(pl.multiple_of(half * ROWS, ROWS), ROWS)
        keys = kk[row].reshape(n_keys, HEAD_DIM)
        values = vv[row].reshape(n_keys, HEAD_DIM)
        s = mm(jnp.concatenate([keys, kaug[row]], axis=1), qt[:, cols], ((1,), (0,)))
        p = jnp.exp2(s * (SCALE * LOG2E))
        if diagonal:
            key_at = lax.broadcasted_iota(jnp.int32, (TOK, ROWS), 0)
            query_at = lax.broadcasted_iota(jnp.int32, (TOK, ROWS), 1) % TOK
            later = (key_at > query_at) & (key_at <= (query_at | (TOK // 2 - 1)))
            p = jnp.concatenate([jnp.where(later, 0.0, p[:TOK]), p[TOK:]], axis=0)
        dp = mm(jnp.concatenate([values, ones], axis=1), dot[:, cols], ((1,), (0,)))
        ds = (p * dp).astype(BF)
        acc[row, 1] += mm(p.astype(BF), dorow[cols, :], ((1,), (0,)))
        acc[row, 0] += mm(ds, qrow[cols, :], ((1,), (0,)))
        dqt[:, cols] += mm(keys, ds, ((0,), (0,)))

    def send_row(row, own):
        for dy in range(1, NY):
            sendbuf[row, dy - 1] = acc[row, :, dy * TOK:(dy + 1) * TOK, :].astype(BF)
            if own:
                for dt in range(NT):
                    own_copy(dy, dt).start()
            else:
                s1_copy(row, dy).start()
        if own:
            s2buf[row] = acc[row, :, :TOK, :].astype(BF)
            for dt in range(1, NT):
                own_copy(0, dt).start()

    def sum_row(row):
        settle(red1.at[row], s1_r.at[row])
        total = acc[row, :, :TOK, :]
        for dy in range(1, NY):
            total = total + red1[row, dy - 1].astype(F32)
        s2buf[row] = total.astype(BF)
        for dt in range(NT):
            s2_copy(row, dt).start()

    order = unit_order()
    rels, halves = [r for r, _ in order], [h for _, h in order]
    seen, done_at = set(), {}
    for at, (rel, _) in enumerate(order):
        if rel in seen:
            done_at[rel] = at
        seen.add(rel)
    finished = sorted(done_at, key=done_at.get)
    first_partner = halves.index(1)
    summed_inside = [rel for rel in finished if rel and done_at[rel] + LAG < len(order)]

    settle(vv.at[z, 1:], vy_r.at[z])
    unit(z, 0, True)

    def send_query_grad(half):
        for h in range(GROUP):
            at = slice(half * ROWS + h * TOK, half * ROWS + (h + 1) * TOK)
            dqs[half, :, h * HEAD_DIM:(h + 1) * HEAD_DIM] = (dqt[:, at].T * SCALE).astype(BF)
        for dt in range(NT):
            if half or dt:
                dq_copy(half, dt).start()
        if not half:
            rdq[0, t] = dqs[0, pl.ds(pl.multiple_of(t * piece, piece), piece), :]

    def step(u, carry):
        row = wrap(z + pick(u, rels), NZ)
        half = pick(u, halves)

        for dist in range(1, NZ // 2 + 1):
            @pl.when(u == rels.index(-dist))
            def _():
                if dist > 1:
                    pass_keys(dist)
                if dist + 1 <= NZ // 2:
                    pass_values(dist + 1)
                for dz in sorted({dist, NZ - dist}):
                    row = wrap(z - dz, NZ)
                    settle(vv.at[row, 1:], vy_r.at[row])

        @pl.when(u == first_partner)
        def _():
            settle(dobuf.at[1], do_r.at[1])
            q_copy().wait_recv()
            ld_copy().wait_recv()
            put_heads(1, q2, qrow, qt)
            put_extra(1, 0, qt, 1.0)
            put_heads(1, dobuf.at[1], dorow, dot)
            put_extra(1, GROUP, dot, 0.0)

        unit(row, half, False)

        @pl.when(u == len(order) - 1 - halves[::-1].index(0))
        def _():
            send_query_grad(0)

        for rel in finished:
            @pl.when(u == done_at[rel])
            def _():
                send_row(wrap(z + rel, NZ), rel == 0)

            if rel in summed_inside:
                @pl.when(u == done_at[rel] + LAG)
                def _():
                    sum_row(wrap(z + rel, NZ))

        return carry

    lax.fori_loop(1, len(order), step, 0)

    send_query_grad(1)
    for rel in finished:
        if rel and rel not in summed_inside:
            sum_row(wrap(z + rel, NZ))
    fin[NZ - 1, t] = s2buf[z, :, pl.ds(pl.multiple_of(t * piece, piece), piece), :]

    if NT > 1:
        settle(rdq.at[0, :NT - 1], dq_r.at[0])
    settle(rdq.at[1], dq_r.at[1])
    for tt in range(NT):
        dq_out[:, tt * ROWS:(tt + 1) * ROWS] = (rdq[0, tt].astype(F32) + rdq[1, tt].astype(F32)).astype(BF)
    if NT > 1:
        settle(fin.at[0, :NT - 1], kv_r.at[0])
    settle(fin.at[NZ:], kv_r.at[1])
    settle(fin.at[:NZ - 1], s2_r.at[0])
    for tt in range(NT):
        total = fin[0, tt].astype(F32)
        for n in range(1, NZ + NY - 1):
            total = total + fin[n, tt].astype(F32)
        dk_out[:, tt * HEAD_DIM:(tt + 1) * HEAD_DIM] = (total[0] * SCALE).astype(BF)
        dv_out[:, tt * HEAD_DIM:(tt + 1) * HEAD_DIM] = total[1].astype(BF)

    if NT > 1:
        settle(dobuf.at[0, :(NT - 1) * piece], do_s.at[0])
        settle(rdq.at[0, :NT - 1], dq_s.at[0])
        settle(fin.at[0, :NT - 1], kv_s.at[0])
    settle(dobuf.at[1], do_s.at[1])
    settle(rdq.at[1], dq_s.at[1])
    settle(kk.at[0, 1:], ky_s.at[0])
    settle(vv.at[1:, 0], vz_s.at[0])
    settle(vv.at[:, 1:], vy_s.at[0])
    settle(kk.at[1:], ring_s.at[0])
    settle(red1.at[1:], s1_s.at[0])
    settle(fin.at[NZ:], kv_s.at[1])
    settle(fin.at[:NZ - 1], s2_s.at[0])
    q_copy().wait_send()
    ld_copy().wait_send()


def per_device(queries, key_rows, value_rows, attn_out, log_norm, grad_out, block_pos):
    piece = TOK // NT
    vmem = pl.BlockSpec(memory_space=pltpu.VMEM)
    dma = pltpu.SemaphoreType.DMA
    blk = (2, TOK, HEAD_DIM)
    return pl.pallas_call(
        kernel,
        out_shape=[
            jax.ShapeDtypeStruct((piece, NT * ROWS), BF),
            jax.ShapeDtypeStruct((piece, NT * HEAD_DIM), BF),
            jax.ShapeDtypeStruct((piece, NT * HEAD_DIM), BF),
        ],
        in_specs=[pl.BlockSpec(memory_space=pltpu.HBM)] * 7,
        out_specs=[vmem] * 3,
        scratch_shapes=[
            pltpu.VMEM((TOK, ROWS), BF),
            pltpu.VMEM((TOK, ROWS), BF),
            pltpu.SMEM((2 * NX * NZ * NY,), jnp.int32),
            pltpu.VMEM((NZ, NY, TOK, HEAD_DIM), BF),
            pltpu.VMEM((NZ, NY, TOK, HEAD_DIM), BF),
            pltpu.VMEM((TOK, ROWS), BF),
            pltpu.VMEM((2, TOK, ROWS), BF),
            pltpu.VMEM((2, 2 * GROUP, TOK), F32),
            pltpu.VMEM((2 * ROWS, HEAD_DIM), BF),
            pltpu.VMEM((2 * ROWS, HEAD_DIM), BF),
            pltpu.VMEM((2 * HEAD_DIM, 2 * ROWS), BF),
            pltpu.VMEM((2 * HEAD_DIM, 2 * ROWS), BF),
            pltpu.VMEM((HEAD_DIM, 2 * ROWS), F32),
            pltpu.VMEM((NZ, 2, NY * TOK, HEAD_DIM), F32),
            pltpu.VMEM((NZ, NY - 1) + blk, BF),
            pltpu.VMEM((NZ, NY - 1) + blk, BF),
            pltpu.VMEM((NZ,) + blk, BF),
            pltpu.VMEM((NZ + NY - 1, NT, 2, piece, HEAD_DIM), BF),
            pltpu.VMEM((2, TOK, ROWS), BF),
            pltpu.VMEM((2, NT, piece, ROWS), BF),
            pltpu.VMEM((NZ, NY * TOK, HEAD_DIM), BF),
            dma((7,)), dma((1,)), dma((1,)), dma((1,)), dma((NZ,)), dma((1,)), dma((NZ,)), dma((2,)), dma((2,)),
            dma((1,)), dma((1,)), dma((1,)), dma((1,)), dma((1,)), dma((NZ,)), dma((1,)), dma((NZ,)),
            dma((1,)), dma((1,)), dma((2,)), dma((2,)), dma((2,)), dma((2,)),
        ],
        compiler_params=pltpu.CompilerParams(
            collective_id=0, has_side_effects=True, vmem_limit_bytes=60 * 2**20
        ),
    )(queries, key_rows, value_rows, attn_out, log_norm.T, grad_out, block_pos)


def solution(mesh):
    split = P("ctx", "tp")
    joint = P(("ctx", "tp"), None)
    return jax.shard_map(
        per_device,
        mesh=mesh,
        in_specs=(split, split, split, split, split, joint, P()),
        out_specs=(joint, joint, joint),
        check_vma=False,
    )
```

```python
import functools

import jax
import jax.numpy as jnp
from jax import lax
from jax.experimental import pallas as pl
from jax.experimental.pallas import tpu as pltpu
from jax.sharding import PartitionSpec as P

MESH = pl.DeviceIdType.MESH
HEAD_DIM = 128
GROUP = 8
TOK = 128
NX, NZ, NY, NT = 2, 8, 4, 4
LAG = 3
ROWS = GROUP * TOK
SCALE = HEAD_DIM ** -0.5
LOG2E = 1.4426950408889634
NEG = -32768.0
BF = jnp.bfloat16
F32 = jnp.float32


def mm(a, b, dims):
    return lax.dot_general(a, b, (dims, ((), ())), preferred_element_type=F32)


def unit_order():
    if NZ != 8:
        rels = [0] + [rel for d in range(1, NZ // 2 + 1) for rel in ((-d, d) if d < NZ // 2 else (-d,))]
        return [(rel, half) for half in range(2) for rel in (rels, rels[::-1])[half]]
    near = [(0, 0), (-1, 0), (1, 0), (-1, 1), (-2, 0), (2, 0), (-2, 1), (2, 1)]
    return near + [(-3, 0), (3, 0), (-3, 1), (3, 1), (-4, 0), (-4, 1), (1, 1), (0, 1)]


def pick(index, table):
    value = jnp.int32(table[0])
    for at, entry in enumerate(table):
        if at:
            value = jnp.where(index == at, jnp.int32(entry), value)
    return value


def split3(x):
    hi = x.astype(BF).astype(F32)
    mid = (x - hi).astype(BF).astype(F32)
    return hi, mid, x - hi - mid


def kernel(
    q_hbm, k_in, v_in, o_hbm, ln_in, do_in, bp_in,
    dq_out, dk_out, dv_out,
    q_in, o_in, bp, kk, vv, q2, dobuf, ld, qrow, dorow, qt, dot, dqt, acc, sendbuf, red1, s2buf, fin, dqs, rdq, kaug,
    loc, ky_s, ky_r, vz_s, vz_r, vy_s, vy_r, do_s, do_r, q_s, q_r, ld_s, ld_r, ring_s, ring_r, s1_s, s1_r, s2_s, s2_r, kv_s, kv_r, dq_s, dq_r,
):
    ctx = lax.axis_index("ctx")
    t = lax.axis_index("tp")
    plane = NZ * NY
    xl = lax.div(ctx, plane)
    z = lax.rem(lax.div(ctx, NY), NZ)
    y = lax.rem(ctx, NY)
    xp = 1 - xl
    piece = TOK // NT

    def dev(x_, z_, y_, t_):
        return (x_ * plane + z_ * NY + y_, t_)

    def wrap(value, count):
        return lax.rem(value + count, count)

    group = [(dx, dt) for dx in range(NX) for dt in range(NT) if dx or dt]

    def group_dev(dx, dt):
        return dev(lax.rem(xl + dx, NX), z, y, lax.rem(t + dt, NT))

    barrier = pltpu.get_barrier_semaphore()
    peers = [group_dev(dx, dt) for dx, dt in group]
    peers += [dev(xl, z, lax.rem(y + dy, NY), t) for dy in range(1, NY)]
    peers += [dev(xl, lax.rem(z + dz, NZ), y, t) for dz in range(1, NZ)]
    next_rows = sorted({1, NZ - 1})
    peers += [dev(xl, lax.rem(z + dz, NZ), lax.rem(y + dy, NY), t) for dz in next_rows for dy in range(1, NY)]
    for peer in peers:
        pl.semaphore_signal(barrier, inc=1, device_id=peer, device_id_type=MESH)

    fetches = [
        pltpu.make_async_copy(src, dst, loc.at[at])
        for at, (src, dst) in enumerate([
            (k_in, kk.at[z, 0]),
            (v_in, vv.at[z, 0]),
            (q_hbm, q_in),
            (ln_in, ld.at[0, :GROUP, :]),
            (bp_in, bp),
            (o_hbm, o_in),
            (
                do_in.at[:, pl.ds(pl.multiple_of(t * ROWS, ROWS), ROWS)],
                dobuf.at[0, pl.ds(pl.multiple_of(t * piece, piece), piece), :],
            ),
        ])
    ]
    for fetch in fetches:
        fetch.start()
    pl.semaphore_wait(barrier, len(peers))

    def copy(src, dst, send, recv, device):
        return pltpu.make_async_remote_copy(
            src_ref=src, dst_ref=dst, send_sem=send, recv_sem=recv, device_id=device, device_id_type=MESH
        )

    def settle(ref, sem):
        pltpu.make_async_copy(ref, ref, sem).wait()

    def do_copy(dx, dt):
        tt = lax.rem(t + dt, NT)
        return copy(
            do_in.at[:, pl.ds(pl.multiple_of(tt * ROWS, ROWS), ROWS)],
            dobuf.at[dx, pl.ds(pl.multiple_of(t * piece, piece), piece), :],
            do_s.at[dx], do_r.at[dx], group_dev(dx, dt),
        )

    def ky_copy(dy):
        return copy(kk.at[z, 0], kk.at[z, dy], ky_s.at[0], ky_r.at[0], dev(xl, z, lax.rem(y + dy, NY), t))

    def vz_copy(dz):
        dist = min(dz, NZ - dz)
        return copy(vv.at[z, 0], vv.at[z, 0], vz_s.at[0], vz_r.at[dist], dev(xl, lax.rem(z + dz, NZ), y, t))

    def vy_copy(row, dy):
        return copy(vv.at[row, 0], vv.at[row, dy], vy_s.at[0], vy_r.at[row], dev(xl, z, lax.rem(y + dy, NY), t))

    def q_copy():
        return copy(q_hbm, q2, q_s.at[0], q_r.at[0], dev(xp, z, y, t))

    def ld_copy():
        return copy(ld.at[0], ld.at[1], ld_s.at[0], ld_r.at[0], dev(xp, z, y, t))

    def next_keys(dz, dy):
        to = dev(xl, lax.rem(z + dz, NZ), lax.rem(y + dy, NY), t)
        return copy(kk.at[z, 0], kk.at[z, dy], ring_s.at[0], ring_r.at[0], to)

    def next_values(dz, dy):
        to = dev(xl, lax.rem(z + dz, NZ), lax.rem(y + dy, NY), t)
        return copy(vv.at[z, 0], vv.at[z, dy], vy_s.at[0], vy_r.at[z], to)

    def ring_copy(step, back):
        row = lax.rem(z + step, NZ) if back else wrap(z - step, NZ)
        to = wrap(z - 1, NZ) if back else lax.rem(z + 1, NZ)
        part = pl.ds(0, NY) if step < NZ // 2 - 1 else pl.ds(back * NY // 2, NY // 2)
        return copy(kk.at[row, part], kk.at[row, part], ring_s.at[0], ring_r.at[step], dev(xl, to, y, t))

    def s1_copy(row, dy):
        return copy(
            sendbuf.at[row, dy - 1], red1.at[row, dy - 1], s1_s.at[0], s1_r.at[row], dev(xl, z, wrap(y - dy, NY), t)
        )

    def s2_copy(row, dt):
        tt = lax.rem(t + dt, NT)
        rows = pl.ds(pl.multiple_of(tt * piece, piece), piece)
        from_there = wrap(z - row, NZ) - 1
        return copy(s2buf.at[row, :, rows, :], fin.at[from_there, t], s2_s.at[0], s2_r.at[0], dev(xl, row, y, tt))

    def own_copy(dy, dt):
        tt = lax.rem(t + dt, NT)
        rows = pl.ds(pl.multiple_of(tt * piece, piece), piece)
        src = sendbuf.at[z, dy - 1, :, rows, :] if dy else s2buf.at[z, :, rows, :]
        n = min(dy, 1)
        return copy(src, fin.at[NZ - 1 + dy, t], kv_s.at[n], kv_r.at[n], dev(xl, z, wrap(y - dy, NY), tt))

    def dq_copy(dx, dt):
        tt = lax.rem(t + dt, NT)
        rows = pl.ds(pl.multiple_of(tt * piece, piece), piece)
        return copy(dqs.at[dx, rows, :], rdq.at[dx, t], dq_s.at[dx], dq_r.at[dx], group_dev(dx, dt))

    for dt in range(1, NT):
        do_copy(0, dt).start()
    fetches[0].wait()
    fetches[1].wait()

    for dy in range(1, NY):
        ky_copy(dy).start()
    near_first = [dz for _, dz in sorted((min(dz, NZ - dz), dz) for dz in range(1, NZ))]
    for dy in range(1, NY):
        vy_copy(z, dy).start()
    for dz in next_rows:
        for dy in range(NY):
            next_keys(dz, dy).start()
    for dz in next_rows:
        vz_copy(dz).start()
        for dy in range(1, NY):
            next_values(dz, dy).start()

    sub16 = lax.broadcasted_iota(jnp.int32, (16, TOK), 0)
    tok16 = lax.broadcasted_iota(jnp.int32, (16, TOK), 1)

    def put_heads(half, src, rows_ref, cols_ref):
        for h in range(GROUP):
            blk = src[:, h * HEAD_DIM:(h + 1) * HEAD_DIM]
            at = slice(half * ROWS + h * TOK, half * ROWS + (h + 1) * TOK)
            rows_ref[at, :] = blk
            cols_ref[:HEAD_DIM, at] = blk.T

    def put_extra(half, base, cols_ref, hot):
        for h in range(GROUP):
            hi, mid, low = split3(ld[half, base + h:base + h + 1, :])
            tile = jnp.where(sub16 == 4 + 2 * half + tok16 // (TOK // 2), hot, 0.0)
            tile = jnp.where(sub16 == 0, hi, jnp.where(sub16 == 1, mid, jnp.where(sub16 == 2, low, tile)))
            at = slice(half * ROWS + h * TOK, half * ROWS + (h + 1) * TOK)
            cols_ref[HEAD_DIM:HEAD_DIM + 16, at] = tile.astype(BF)

    acc[...] = jnp.zeros_like(acc)
    dqt[...] = jnp.zeros_like(dqt)
    qt[HEAD_DIM:, :] = jnp.zeros_like(qt[HEAD_DIM:, :])
    dot[HEAD_DIM:, :] = jnp.zeros_like(dot[HEAD_DIM:, :])
    for fetch in fetches[2:5]:
        fetch.wait()
    ld[0, :GROUP, :] = ld[0, :GROUP, :] * (-1.0 / SCALE)
    put_heads(0, q_in, qrow, qt)
    put_extra(0, 0, qt, 1.0)

    lane = lax.broadcasted_iota(jnp.int32, (1, HEAD_DIM), 1)
    here, there = 2 * ctx, 2 * (xp * plane + z * NY + y)
    limit = jnp.full((1, HEAD_DIM), 1 << 20, jnp.int32)
    for at, half_block in enumerate((here, here + 1, there, there + 1)):
        limit = jnp.where(lane == 4 + at, bp[half_block], limit)

    def put_kaug(row, carry):
        for yy in range(NY):
            for hf in range(2):
                place = bp[2 * (xl * plane + row * NY + wrap(y - yy, NY)) + hf]
                line = jnp.where(lane < 3, 1.0, jnp.where(place > limit, NEG, 0.0))
                kaug[row, yy * TOK + hf * (TOK // 2):yy * TOK + (hf + 1) * (TOK // 2), :] = jnp.broadcast_to(
                    line, (TOK // 2, HEAD_DIM)
                ).astype(BF)
        return carry

    lax.fori_loop(0, NZ, put_kaug, 0)
    for dt in range(NT):
        do_copy(1, dt).start()
    q_copy().start()
    for dz in near_first[len(next_rows):]:
        vz_copy(dz).start()

    settle(kk.at[z, 1:], ky_r.at[0])

    def pass_values(dist):
        both = sorted({dist, NZ - dist})
        settle(vv.at[:len(both), 0], vz_r.at[dist])
        for dz in both:
            if dist > 1:
                for dy in range(1, NY):
                    vy_copy(wrap(z - dz, NZ), dy).start()

    def pass_keys(dist):
        settle(kk.at[:2 if dist < NZ // 2 else 1], ring_r.at[dist - 1])
        if dist < NZ // 2:
            ring_copy(dist, 0).start()
            ring_copy(dist, 1).start()

    pass_values(1)
    pass_keys(1)
    for fetch in fetches[5:]:
        fetch.wait()
    if NT > 1:
        settle(dobuf.at[0, :(NT - 1) * piece], do_r.at[0])
    put_heads(0, dobuf.at[0], dorow, dot)
    for h in range(GROUP):
        out_t = o_in[:, h * HEAD_DIM:(h + 1) * HEAD_DIM].T.astype(F32)
        grad_t = dot[:HEAD_DIM, h * TOK:(h + 1) * TOK].astype(F32)
        ld[0, GROUP + h:GROUP + h + 1, :] = -jnp.sum(out_t * grad_t, axis=0, keepdims=True)
    ld_copy().start()
    put_extra(0, GROUP, dot, 0.0)

    n_keys = NY * TOK
    ones = jnp.where(lax.broadcasted_iota(jnp.int32, (n_keys, HEAD_DIM), 1) < 3, 1.0, 0.0).astype(BF)

    def unit(row, half, diagonal):
        cols = pl.ds(pl.multiple_of(half * ROWS, ROWS), ROWS)
        keys = kk[row].reshape(n_keys, HEAD_DIM)
        values = vv[row].reshape(n_keys, HEAD_DIM)
        s = mm(jnp.concatenate([keys, kaug[row]], axis=1), qt[:, cols], ((1,), (0,)))
        p = jnp.exp2(s * (SCALE * LOG2E))
        if diagonal:
            key_at = lax.broadcasted_iota(jnp.int32, (TOK, ROWS), 0)
            query_at = lax.broadcasted_iota(jnp.int32, (TOK, ROWS), 1) % TOK
            later = (key_at > query_at) & (key_at <= (query_at | (TOK // 2 - 1)))
            p = jnp.concatenate([jnp.where(later, 0.0, p[:TOK]), p[TOK:]], axis=0)
        dp = mm(jnp.concatenate([values, ones], axis=1), dot[:, cols], ((1,), (0,)))
        ds = (p * dp).astype(BF)
        acc[row, 1] += mm(p.astype(BF), dorow[cols, :], ((1,), (0,)))
        acc[row, 0] += mm(ds, qrow[cols, :], ((1,), (0,)))
        dqt[:, cols] += mm(keys, ds, ((0,), (0,)))

    def send_row(row, own):
        for dy in range(1, NY):
            sendbuf[row, dy - 1] = acc[row, :, dy * TOK:(dy + 1) * TOK, :].astype(BF)
            if own:
                for dt in range(NT):
                    own_copy(dy, dt).start()
            else:
                s1_copy(row, dy).start()
        if own:
            s2buf[row] = acc[row, :, :TOK, :].astype(BF)
            for dt in range(1, NT):
                own_copy(0, dt).start()

    def sum_row(row):
        settle(red1.at[row], s1_r.at[row])
        total = acc[row, :, :TOK, :]
        for dy in range(1, NY):
            total = total + red1[row, dy - 1].astype(F32)
        s2buf[row] = total.astype(BF)
        for dt in range(NT):
            s2_copy(row, dt).start()

    order = unit_order()
    rels, halves = [r for r, _ in order], [h for _, h in order]
    seen, done_at = set(), {}
    for at, (rel, _) in enumerate(order):
        if rel in seen:
            done_at[rel] = at
        seen.add(rel)
    finished = sorted(done_at, key=done_at.get)
    first_partner = halves.index(1)
    summed_inside = [rel for rel in finished if rel and done_at[rel] + LAG < len(order)]

    settle(vv.at[z, 1:], vy_r.at[z])
    unit(z, 0, True)

    def send_query_grad(half):
        for h in range(GROUP):
            at = slice(half * ROWS + h * TOK, half * ROWS + (h + 1) * TOK)
            dqs[half, :, h * HEAD_DIM:(h + 1) * HEAD_DIM] = (dqt[:, at].T * SCALE).astype(BF)
        for dt in range(NT):
            if half or dt:
                dq_copy(half, dt).start()
        if not half:
            rdq[0, t] = dqs[0, pl.ds(pl.multiple_of(t * piece, piece), piece), :]

    def step(u, carry):
        row = wrap(z + pick(u, rels), NZ)
        half = pick(u, halves)

        for dist in range(1, NZ // 2 + 1):
            @pl.when(u == rels.index(-dist))
            def _():
                if dist > 1:
                    pass_keys(dist)
                if dist + 1 <= NZ // 2:
                    pass_values(dist + 1)
                for dz in sorted({dist, NZ - dist}):
                    row = wrap(z - dz, NZ)
                    settle(vv.at[row, 1:], vy_r.at[row])

        @pl.when(u == first_partner)
        def _():
            settle(dobuf.at[1], do_r.at[1])
            q_copy().wait_recv()
            ld_copy().wait_recv()
            put_heads(1, q2, qrow, qt)
            put_extra(1, 0, qt, 1.0)
            put_heads(1, dobuf.at[1], dorow, dot)
            put_extra(1, GROUP, dot, 0.0)

        unit(row, half, False)

        @pl.when(u == len(order) - 1 - halves[::-1].index(0))
        def _():
            send_query_grad(0)

        for rel in finished:
            @pl.when(u == done_at[rel])
            def _():
                send_row(wrap(z + rel, NZ), rel == 0)

            if rel in summed_inside:
                @pl.when(u == done_at[rel] + LAG)
                def _():
                    sum_row(wrap(z + rel, NZ))

        return carry

    lax.fori_loop(1, len(order), step, 0)

    send_query_grad(1)
    for rel in finished:
        if rel and rel not in summed_inside:
            sum_row(wrap(z + rel, NZ))
    fin[NZ - 1, t] = s2buf[z, :, pl.ds(pl.multiple_of(t * piece, piece), piece), :]

    if NT > 1:
        settle(rdq.at[0, :NT - 1], dq_r.at[0])
    settle(rdq.at[1], dq_r.at[1])
    for tt in range(NT):
        dq_out[:, tt * ROWS:(tt + 1) * ROWS] = (rdq[0, tt].astype(F32) + rdq[1, tt].astype(F32)).astype(BF)
    if NT > 1:
        settle(fin.at[0, :NT - 1], kv_r.at[0])
    settle(fin.at[NZ:], kv_r.at[1])
    settle(fin.at[:NZ - 1], s2_r.at[0])
    for tt in range(NT):
        total = fin[0, tt].astype(F32)
        for n in range(1, NZ + NY - 1):
            total = total + fin[n, tt].astype(F32)
        dk_out[:, tt * HEAD_DIM:(tt + 1) * HEAD_DIM] = (total[0] * SCALE).astype(BF)
        dv_out[:, tt * HEAD_DIM:(tt + 1) * HEAD_DIM] = total[1].astype(BF)

    if NT > 1:
        settle(dobuf.at[0, :(NT - 1) * piece], do_s.at[0])
        settle(rdq.at[0, :NT - 1], dq_s.at[0])
        settle(fin.at[0, :NT - 1], kv_s.at[0])
    settle(dobuf.at[1], do_s.at[1])
    settle(rdq.at[1], dq_s.at[1])
    settle(kk.at[0, 1:], ky_s.at[0])
    settle(vv.at[1:, 0], vz_s.at[0])
    settle(vv.at[:, 1:], vy_s.at[0])
    settle(kk.at[1:], ring_s.at[0])
    settle(red1.at[1:], s1_s.at[0])
    settle(fin.at[NZ:], kv_s.at[1])
    settle(fin.at[:NZ - 1], s2_s.at[0])
    q_copy().wait_send()
    ld_copy().wait_send()


def per_device(queries, key_rows, value_rows, attn_out, log_norm, grad_out, block_pos):
    piece = TOK // NT
    vmem = pl.BlockSpec(memory_space=pltpu.VMEM)
    dma = pltpu.SemaphoreType.DMA
    blk = (2, TOK, HEAD_DIM)
    return pl.pallas_call(
        kernel,
        out_shape=[
            jax.ShapeDtypeStruct((piece, NT * ROWS), BF),
            jax.ShapeDtypeStruct((piece, NT * HEAD_DIM), BF),
            jax.ShapeDtypeStruct((piece, NT * HEAD_DIM), BF),
        ],
        in_specs=[pl.BlockSpec(memory_space=pltpu.HBM)] * 7,
        out_specs=[vmem] * 3,
        scratch_shapes=[
            pltpu.VMEM((TOK, ROWS), BF),
            pltpu.VMEM((TOK, ROWS), BF),
            pltpu.SMEM((2 * NX * NZ * NY,), jnp.int32),
            pltpu.VMEM((NZ, NY, TOK, HEAD_DIM), BF),
            pltpu.VMEM((NZ, NY, TOK, HEAD_DIM), BF),
            pltpu.VMEM((TOK, ROWS), BF),
            pltpu.VMEM((2, TOK, ROWS), BF),
            pltpu.VMEM((2, 2 * GROUP, TOK), F32),
            pltpu.VMEM((2 * ROWS, HEAD_DIM), BF),
            pltpu.VMEM((2 * ROWS, HEAD_DIM), BF),
            pltpu.VMEM((2 * HEAD_DIM, 2 * ROWS), BF),
            pltpu.VMEM((2 * HEAD_DIM, 2 * ROWS), BF),
            pltpu.VMEM((HEAD_DIM, 2 * ROWS), F32),
            pltpu.VMEM((NZ, 2, NY * TOK, HEAD_DIM), F32),
            pltpu.VMEM((NZ, NY - 1) + blk, BF),
            pltpu.VMEM((NZ, NY - 1) + blk, BF),
            pltpu.VMEM((NZ,) + blk, BF),
            pltpu.VMEM((NZ + NY - 1, NT, 2, piece, HEAD_DIM), BF),
            pltpu.VMEM((2, TOK, ROWS), BF),
            pltpu.VMEM((2, NT, piece, ROWS), BF),
            pltpu.VMEM((NZ, NY * TOK, HEAD_DIM), BF),
            dma((7,)), dma((1,)), dma((1,)), dma((1,)), dma((NZ,)), dma((1,)), dma((NZ,)), dma((2,)), dma((2,)),
            dma((1,)), dma((1,)), dma((1,)), dma((1,)), dma((1,)), dma((NZ,)), dma((1,)), dma((NZ,)),
            dma((1,)), dma((1,)), dma((2,)), dma((2,)), dma((2,)), dma((2,)),
        ],
        compiler_params=pltpu.CompilerParams(
            collective_id=0, has_side_effects=True, vmem_limit_bytes=60 * 2**20
        ),
    )(queries, key_rows, value_rows, attn_out, log_norm.T, grad_out, block_pos)


def solution(mesh):
    split = P("ctx", "tp")
    joint = P(("ctx", "tp"), None)
    return jax.shard_map(
        per_device,
        mesh=mesh,
        in_specs=(split, split, split, split, split, joint, P()),
        out_specs=(joint, joint, joint),
        check_vma=False,
    )
```

```python
import functools

import jax
import jax.numpy as jnp
from jax import lax
from jax.experimental import pallas as pl
from jax.experimental.pallas import tpu as pltpu
from jax.sharding import PartitionSpec as P

MESH = pl.DeviceIdType.MESH
HEAD_DIM = 128
GROUP = 8
TOK = 128
NX, NZ, NY, NT = 2, 8, 4, 4
LAG = 3
ROWS = GROUP * TOK
SCALE = HEAD_DIM ** -0.5
LOG2E = 1.4426950408889634
NEG = -32768.0
BF = jnp.bfloat16
F32 = jnp.float32


def mm(a, b, dims):
    return lax.dot_general(a, b, (dims, ((), ())), preferred_element_type=F32)


def unit_order():
    if NZ != 8:
        rels = [0] + [rel for d in range(1, NZ // 2 + 1) for rel in ((-d, d) if d < NZ // 2 else (-d,))]
        return [(rel, half) for half in range(2) for rel in (rels, rels[::-1])[half]]
    near = [(0, 0), (-1, 0), (1, 0), (-1, 1), (-2, 0), (2, 0), (-2, 1), (2, 1)]
    return near + [(-3, 0), (3, 0), (-3, 1), (3, 1), (-4, 0), (-4, 1), (1, 1), (0, 1)]


def pick(index, table):
    value = jnp.int32(table[0])
    for at, entry in enumerate(table):
        if at:
            value = jnp.where(index == at, jnp.int32(entry), value)
    return value


def split3(x):
    hi = x.astype(BF).astype(F32)
    mid = (x - hi).astype(BF).astype(F32)
    return hi, mid, x - hi - mid


def kernel(
    q_hbm, k_in, v_in, o_hbm, ln_in, do_in, bp_in,
    dq_out, dk_out, dv_out,
    q_in, o_in, bp, kk, vv, q2, dobuf, ld, qrow, dorow, qt, dot, dqt, acc, sendbuf, red1, s2buf, fin, dqs, rdq, kaug,
    loc, ky_s, ky_r, vz_s, vz_r, vy_s, vy_r, do_s, do_r, q_s, q_r, ld_s, ld_r, ring_s, ring_r, s1_s, s1_r, s2_s, s2_r, kv_s, kv_r, dq_s, dq_r,
):
    ctx = lax.axis_index("ctx")
    t = lax.axis_index("tp")
    plane = NZ * NY
    xl = lax.div(ctx, plane)
    z = lax.rem(lax.div(ctx, NY), NZ)
    y = lax.rem(ctx, NY)
    xp = 1 - xl
    piece = TOK // NT

    def dev(x_, z_, y_, t_):
        return (x_ * plane + z_ * NY + y_, t_)

    def wrap(value, count):
        return lax.rem(value + count, count)

    group = [(dx, dt) for dx in range(NX) for dt in range(NT) if dx or dt]

    def group_dev(dx, dt):
        return dev(lax.rem(xl + dx, NX), z, y, lax.rem(t + dt, NT))

    barrier = pltpu.get_barrier_semaphore()
    peers = [group_dev(dx, dt) for dx, dt in group]
    peers += [dev(xl, z, lax.rem(y + dy, NY), t) for dy in range(1, NY)]
    peers += [dev(xl, lax.rem(z + dz, NZ), y, t) for dz in range(1, NZ)]
    next_rows = sorted({1, NZ - 1})
    peers += [dev(xl, lax.rem(z + dz, NZ), lax.rem(y + dy, NY), t) for dz in next_rows for dy in range(1, NY)]

    fetches = [
        pltpu.make_async_copy(src, dst, loc.at[at])
        for at, (src, dst) in enumerate([
            (k_in, kk.at[z, 0]),
            (v_in, vv.at[z, 0]),
            (q_hbm, q_in),
            (ln_in, ld.at[0, :GROUP, :]),
            (bp_in, bp),
            (o_hbm, o_in),
            (
                do_in.at[:, pl.ds(pl.multiple_of(t * ROWS, ROWS), ROWS)],
                dobuf.at[0, pl.ds(pl.multiple_of(t * piece, piece), piece), :],
            ),
        ])
    ]
    for fetch in fetches:
        fetch.start()
    for peer in peers:
        pl.semaphore_signal(barrier, inc=1, device_id=peer, device_id_type=MESH)
    pl.semaphore_wait(barrier, len(peers))

    def copy(src, dst, send, recv, device):
        return pltpu.make_async_remote_copy(
            src_ref=src, dst_ref=dst, send_sem=send, recv_sem=recv, device_id=device, device_id_type=MESH
        )

    def settle(ref, sem):
        pltpu.make_async_copy(ref, ref, sem).wait()

    def do_copy(dx, dt):
        tt = lax.rem(t + dt, NT)
        return copy(
            do_in.at[:, pl.ds(pl.multiple_of(tt * ROWS, ROWS), ROWS)],
            dobuf.at[dx, pl.ds(pl.multiple_of(t * piece, piece), piece), :],
            do_s.at[dx], do_r.at[dx], group_dev(dx, dt),
        )

    def ky_copy(dy):
        return copy(kk.at[z, 0], kk.at[z, dy], ky_s.at[0], ky_r.at[0], dev(xl, z, lax.rem(y + dy, NY), t))

    def vz_copy(dz):
        dist = min(dz, NZ - dz)
        return copy(vv.at[z, 0], vv.at[z, 0], vz_s.at[0], vz_r.at[dist], dev(xl, lax.rem(z + dz, NZ), y, t))

    def vy_copy(row, dy):
        return copy(vv.at[row, 0], vv.at[row, dy], vy_s.at[0], vy_r.at[row], dev(xl, z, lax.rem(y + dy, NY), t))

    def q_copy():
        return copy(q_hbm, q2, q_s.at[0], q_r.at[0], dev(xp, z, y, t))

    def ld_copy():
        return copy(ld.at[0], ld.at[1], ld_s.at[0], ld_r.at[0], dev(xp, z, y, t))

    def next_keys(dz, dy):
        to = dev(xl, lax.rem(z + dz, NZ), lax.rem(y + dy, NY), t)
        return copy(kk.at[z, 0], kk.at[z, dy], ring_s.at[0], ring_r.at[0], to)

    def next_values(dz, dy):
        to = dev(xl, lax.rem(z + dz, NZ), lax.rem(y + dy, NY), t)
        return copy(vv.at[z, 0], vv.at[z, dy], vy_s.at[0], vy_r.at[z], to)

    def ring_copy(step, back):
        row = lax.rem(z + step, NZ) if back else wrap(z - step, NZ)
        to = wrap(z - 1, NZ) if back else lax.rem(z + 1, NZ)
        part = pl.ds(0, NY) if step < NZ // 2 - 1 else pl.ds(back * NY // 2, NY // 2)
        return copy(kk.at[row, part], kk.at[row, part], ring_s.at[0], ring_r.at[step], dev(xl, to, y, t))

    def s1_copy(row, dy):
        return copy(
            sendbuf.at[row, dy - 1], red1.at[row, dy - 1], s1_s.at[0], s1_r.at[row], dev(xl, z, wrap(y - dy, NY), t)
        )

    def s2_copy(row, dt):
        tt = lax.rem(t + dt, NT)
        rows = pl.ds(pl.multiple_of(tt * piece, piece), piece)
        from_there = wrap(z - row, NZ) - 1
        return copy(s2buf.at[row, :, rows, :], fin.at[from_there, t], s2_s.at[0], s2_r.at[0], dev(xl, row, y, tt))

    def own_copy(dy, dt):
        tt = lax.rem(t + dt, NT)
        rows = pl.ds(pl.multiple_of(tt * piece, piece), piece)
        src = sendbuf.at[z, dy - 1, :, rows, :] if dy else s2buf.at[z, :, rows, :]
        n = min(dy, 1)
        return copy(src, fin.at[NZ - 1 + dy, t], kv_s.at[n], kv_r.at[n], dev(xl, z, wrap(y - dy, NY), tt))

    def dq_copy(dx, dt):
        tt = lax.rem(t + dt, NT)
        rows = pl.ds(pl.multiple_of(tt * piece, piece), piece)
        return copy(dqs.at[dx, rows, :], rdq.at[dx, t], dq_s.at[dx], dq_r.at[dx], group_dev(dx, dt))

    for dt in range(1, NT):
        do_copy(0, dt).start()
    fetches[0].wait()
    fetches[1].wait()

    for dy in range(1, NY):
        ky_copy(dy).start()
    near_first = [dz for _, dz in sorted((min(dz, NZ - dz), dz) for dz in range(1, NZ))]
    for dy in range(1, NY):
        vy_copy(z, dy).start()
    for dz in next_rows:
        for dy in range(NY):
            next_keys(dz, dy).start()
    for dz in next_rows:
        vz_copy(dz).start()
        for dy in range(1, NY):
            next_values(dz, dy).start()

    sub16 = lax.broadcasted_iota(jnp.int32, (16, TOK), 0)
    tok16 = lax.broadcasted_iota(jnp.int32, (16, TOK), 1)

    def put_heads(half, src, rows_ref, cols_ref):
        for h in range(GROUP):
            blk = src[:, h * HEAD_DIM:(h + 1) * HEAD_DIM]
            at = slice(half * ROWS + h * TOK, half * ROWS + (h + 1) * TOK)
            rows_ref[at, :] = blk
            cols_ref[:HEAD_DIM, at] = blk.T

    def put_extra(half, base, cols_ref, hot):
        for h in range(GROUP):
            hi, mid, low = split3(ld[half, base + h:base + h + 1, :])
            tile = jnp.where(sub16 == 4 + 2 * half + tok16 // (TOK // 2), hot, 0.0)
            tile = jnp.where(sub16 == 0, hi, jnp.where(sub16 == 1, mid, jnp.where(sub16 == 2, low, tile)))
            at = slice(half * ROWS + h * TOK, half * ROWS + (h + 1) * TOK)
            cols_ref[HEAD_DIM:HEAD_DIM + 16, at] = tile.astype(BF)

    acc[...] = jnp.zeros_like(acc)
    dqt[...] = jnp.zeros_like(dqt)
    qt[HEAD_DIM:, :] = jnp.zeros_like(qt[HEAD_DIM:, :])
    dot[HEAD_DIM:, :] = jnp.zeros_like(dot[HEAD_DIM:, :])
    for fetch in fetches[2:5]:
        fetch.wait()
    ld[0, :GROUP, :] = ld[0, :GROUP, :] * (-1.0 / SCALE)
    put_heads(0, q_in, qrow, qt)
    put_extra(0, 0, qt, 1.0)

    lane = lax.broadcasted_iota(jnp.int32, (1, HEAD_DIM), 1)
    here, there = 2 * ctx, 2 * (xp * plane + z * NY + y)
    limit = jnp.full((1, HEAD_DIM), 1 << 20, jnp.int32)
    for at, half_block in enumerate((here, here + 1, there, there + 1)):
        limit = jnp.where(lane == 4 + at, bp[half_block], limit)

    def put_kaug(row, carry):
        for yy in range(NY):
            for hf in range(2):
                place = bp[2 * (xl * plane + row * NY + wrap(y - yy, NY)) + hf]
                line = jnp.where(lane < 3, 1.0, jnp.where(place > limit, NEG, 0.0))
                kaug[row, yy * TOK + hf * (TOK // 2):yy * TOK + (hf + 1) * (TOK // 2), :] = jnp.broadcast_to(
                    line, (TOK // 2, HEAD_DIM)
                ).astype(BF)
        return carry

    lax.fori_loop(0, NZ, put_kaug, 0)
    for dt in range(NT):
        do_copy(1, dt).start()
    q_copy().start()
    for dz in near_first[len(next_rows):]:
        vz_copy(dz).start()

    settle(kk.at[z, 1:], ky_r.at[0])

    def pass_values(dist):
        both = sorted({dist, NZ - dist})
        settle(vv.at[:len(both), 0], vz_r.at[dist])
        for dz in both:
            if dist > 1:
                for dy in range(1, NY):
                    vy_copy(wrap(z - dz, NZ), dy).start()

    def pass_keys(dist):
        settle(kk.at[:2 if dist < NZ // 2 else 1], ring_r.at[dist - 1])
        if dist < NZ // 2:
            ring_copy(dist, 0).start()
            ring_copy(dist, 1).start()

    pass_values(1)
    pass_keys(1)
    for fetch in fetches[5:]:
        fetch.wait()
    if NT > 1:
        settle(dobuf.at[0, :(NT - 1) * piece], do_r.at[0])
    put_heads(0, dobuf.at[0], dorow, dot)
    for h in range(GROUP):
        out_t = o_in[:, h * HEAD_DIM:(h + 1) * HEAD_DIM].T.astype(F32)
        grad_t = dot[:HEAD_DIM, h * TOK:(h + 1) * TOK].astype(F32)
        ld[0, GROUP + h:GROUP + h + 1, :] = -jnp.sum(out_t * grad_t, axis=0, keepdims=True)
    ld_copy().start()
    put_extra(0, GROUP, dot, 0.0)

    n_keys = NY * TOK
    ones = jnp.where(lax.broadcasted_iota(jnp.int32, (n_keys, HEAD_DIM), 1) < 3, 1.0, 0.0).astype(BF)

    def unit(row, half, diagonal):
        cols = pl.ds(pl.multiple_of(half * ROWS, ROWS), ROWS)
        keys = kk[row].reshape(n_keys, HEAD_DIM)
        values = vv[row].reshape(n_keys, HEAD_DIM)
        s = mm(jnp.concatenate([keys, kaug[row]], axis=1), qt[:, cols], ((1,), (0,)))
        p = jnp.exp2(s * (SCALE * LOG2E))
        if diagonal:
            key_at = lax.broadcasted_iota(jnp.int32, (TOK, ROWS), 0)
            query_at = lax.broadcasted_iota(jnp.int32, (TOK, ROWS), 1) % TOK
            later = (key_at > query_at) & (key_at <= (query_at | (TOK // 2 - 1)))
            p = jnp.concatenate([jnp.where(later, 0.0, p[:TOK]), p[TOK:]], axis=0)
        dp = mm(jnp.concatenate([values, ones], axis=1), dot[:, cols], ((1,), (0,)))
        ds = (p * dp).astype(BF)
        acc[row, 1] += mm(p.astype(BF), dorow[cols, :], ((1,), (0,)))
        acc[row, 0] += mm(ds, qrow[cols, :], ((1,), (0,)))
        dqt[:, cols] += mm(keys, ds, ((0,), (0,)))

    def send_row(row, own):
        for dy in range(1, NY):
            sendbuf[row, dy - 1] = acc[row, :, dy * TOK:(dy + 1) * TOK, :].astype(BF)
            if own:
                for dt in range(NT):
                    own_copy(dy, dt).start()
            else:
                s1_copy(row, dy).start()
        if own:
            s2buf[row] = acc[row, :, :TOK, :].astype(BF)
            for dt in range(1, NT):
                own_copy(0, dt).start()

    def sum_row(row):
        settle(red1.at[row], s1_r.at[row])
        total = acc[row, :, :TOK, :]
        for dy in range(1, NY):
            total = total + red1[row, dy - 1].astype(F32)
        s2buf[row] = total.astype(BF)
        for dt in range(NT):
            s2_copy(row, dt).start()

    order = unit_order()
    rels, halves = [r for r, _ in order], [h for _, h in order]
    seen, done_at = set(), {}
    for at, (rel, _) in enumerate(order):
        if rel in seen:
            done_at[rel] = at
        seen.add(rel)
    finished = sorted(done_at, key=done_at.get)
    first_partner = halves.index(1)
    summed_inside = [rel for rel in finished if rel and done_at[rel] + LAG < len(order)]

    settle(vv.at[z, 1:], vy_r.at[z])
    unit(z, 0, True)

    def send_query_grad(half):
        for h in range(GROUP):
            at = slice(half * ROWS + h * TOK, half * ROWS + (h + 1) * TOK)
            dqs[half, :, h * HEAD_DIM:(h + 1) * HEAD_DIM] = (dqt[:, at].T * SCALE).astype(BF)
        for dt in range(NT):
            if half or dt:
                dq_copy(half, dt).start()
        if not half:
            rdq[0, t] = dqs[0, pl.ds(pl.multiple_of(t * piece, piece), piece), :]

    def step(u, carry):
        row = wrap(z + pick(u, rels), NZ)
        half = pick(u, halves)

        for dist in range(1, NZ // 2 + 1):
            @pl.when(u == rels.index(-dist))
            def _():
                if dist > 1:
                    pass_keys(dist)
                if dist + 1 <= NZ // 2:
                    pass_values(dist + 1)
                for dz in sorted({dist, NZ - dist}):
                    row = wrap(z - dz, NZ)
                    settle(vv.at[row, 1:], vy_r.at[row])

        @pl.when(u == first_partner)
        def _():
            settle(dobuf.at[1], do_r.at[1])
            q_copy().wait_recv()
            ld_copy().wait_recv()
            put_heads(1, q2, qrow, qt)
            put_extra(1, 0, qt, 1.0)
            put_heads(1, dobuf.at[1], dorow, dot)
            put_extra(1, GROUP, dot, 0.0)

        unit(row, half, False)

        @pl.when(u == len(order) - 1 - halves[::-1].index(0))
        def _():
            send_query_grad(0)

        for rel in finished:
            @pl.when(u == done_at[rel])
            def _():
                send_row(wrap(z + rel, NZ), rel == 0)

            if rel in summed_inside:
                @pl.when(u == done_at[rel] + LAG)
                def _():
                    sum_row(wrap(z + rel, NZ))

        return carry

    lax.fori_loop(1, len(order), step, 0)

    send_query_grad(1)
    for rel in finished:
        if rel and rel not in summed_inside:
            sum_row(wrap(z + rel, NZ))
    fin[NZ - 1, t] = s2buf[z, :, pl.ds(pl.multiple_of(t * piece, piece), piece), :]

    if NT > 1:
        settle(rdq.at[0, :NT - 1], dq_r.at[0])
    settle(rdq.at[1], dq_r.at[1])
    for tt in range(NT):
        dq_out[:, tt * ROWS:(tt + 1) * ROWS] = (rdq[0, tt].astype(F32) + rdq[1, tt].astype(F32)).astype(BF)
    if NT > 1:
        settle(fin.at[0, :NT - 1], kv_r.at[0])
    settle(fin.at[NZ:], kv_r.at[1])
    settle(fin.at[:NZ - 1], s2_r.at[0])
    for tt in range(NT):
        total = fin[0, tt].astype(F32)
        for n in range(1, NZ + NY - 1):
            total = total + fin[n, tt].astype(F32)
        dk_out[:, tt * HEAD_DIM:(tt + 1) * HEAD_DIM] = (total[0] * SCALE).astype(BF)
        dv_out[:, tt * HEAD_DIM:(tt + 1) * HEAD_DIM] = total[1].astype(BF)

    if NT > 1:
        settle(dobuf.at[0, :(NT - 1) * piece], do_s.at[0])
        settle(rdq.at[0, :NT - 1], dq_s.at[0])
        settle(fin.at[0, :NT - 1], kv_s.at[0])
    settle(dobuf.at[1], do_s.at[1])
    settle(rdq.at[1], dq_s.at[1])
    settle(kk.at[0, 1:], ky_s.at[0])
    settle(vv.at[1:, 0], vz_s.at[0])
    settle(vv.at[:, 1:], vy_s.at[0])
    settle(kk.at[1:], ring_s.at[0])
    settle(red1.at[1:], s1_s.at[0])
    settle(fin.at[NZ:], kv_s.at[1])
    settle(fin.at[:NZ - 1], s2_s.at[0])
    q_copy().wait_send()
    ld_copy().wait_send()


def per_device(queries, key_rows, value_rows, attn_out, log_norm, grad_out, block_pos):
    piece = TOK // NT
    vmem = pl.BlockSpec(memory_space=pltpu.VMEM)
    dma = pltpu.SemaphoreType.DMA
    blk = (2, TOK, HEAD_DIM)
    return pl.pallas_call(
        kernel,
        out_shape=[
            jax.ShapeDtypeStruct((piece, NT * ROWS), BF),
            jax.ShapeDtypeStruct((piece, NT * HEAD_DIM), BF),
            jax.ShapeDtypeStruct((piece, NT * HEAD_DIM), BF),
        ],
        in_specs=[pl.BlockSpec(memory_space=pltpu.HBM)] * 7,
        out_specs=[vmem] * 3,
        scratch_shapes=[
            pltpu.VMEM((TOK, ROWS), BF),
            pltpu.VMEM((TOK, ROWS), BF),
            pltpu.SMEM((2 * NX * NZ * NY,), jnp.int32),
            pltpu.VMEM((NZ, NY, TOK, HEAD_DIM), BF),
            pltpu.VMEM((NZ, NY, TOK, HEAD_DIM), BF),
            pltpu.VMEM((TOK, ROWS), BF),
            pltpu.VMEM((2, TOK, ROWS), BF),
            pltpu.VMEM((2, 2 * GROUP, TOK), F32),
            pltpu.VMEM((2 * ROWS, HEAD_DIM), BF),
            pltpu.VMEM((2 * ROWS, HEAD_DIM), BF),
            pltpu.VMEM((2 * HEAD_DIM, 2 * ROWS), BF),
            pltpu.VMEM((2 * HEAD_DIM, 2 * ROWS), BF),
            pltpu.VMEM((HEAD_DIM, 2 * ROWS), F32),
            pltpu.VMEM((NZ, 2, NY * TOK, HEAD_DIM), F32),
            pltpu.VMEM((NZ, NY - 1) + blk, BF),
            pltpu.VMEM((NZ, NY - 1) + blk, BF),
            pltpu.VMEM((NZ,) + blk, BF),
            pltpu.VMEM((NZ + NY - 1, NT, 2, piece, HEAD_DIM), BF),
            pltpu.VMEM((2, TOK, ROWS), BF),
            pltpu.VMEM((2, NT, piece, ROWS), BF),
            pltpu.VMEM((NZ, NY * TOK, HEAD_DIM), BF),
            dma((7,)), dma((1,)), dma((1,)), dma((1,)), dma((NZ,)), dma((1,)), dma((NZ,)), dma((2,)), dma((2,)),
            dma((1,)), dma((1,)), dma((1,)), dma((1,)), dma((1,)), dma((NZ,)), dma((1,)), dma((NZ,)),
            dma((1,)), dma((1,)), dma((2,)), dma((2,)), dma((2,)), dma((2,)),
        ],
        compiler_params=pltpu.CompilerParams(
            collective_id=0, has_side_effects=True, vmem_limit_bytes=60 * 2**20
        ),
    )(queries, key_rows, value_rows, attn_out, log_norm.T, grad_out, block_pos)


def solution(mesh):
    split = P("ctx", "tp")
    joint = P(("ctx", "tp"), None)
    return jax.shard_map(
        per_device,
        mesh=mesh,
        in_specs=(split, split, split, split, split, joint, P()),
        out_specs=(joint, joint, joint),
        check_vma=False,
    )
```
